32 devices in a mesh: box: 8 (over z, x), dir: 4 (over y, core).
Axes of the slice: x: 2, y: 2, z: 4, core: 2. Of those that a mesh axis runs over, the one named last changes fastest.
Arguments:
- child_pat: bfloat16 [4096, 2, 8, 2048], P('box', None, None, 'dir'), may hold values from -6 to 6
- interp: bfloat16 [64, 4, 128, 128], P('dir'), may hold values from -0.25 to 0.25
- interp_blocks: int32 [64, 4], P('dir'), may hold values from 0 to 15, as said below
- shift_angle: float32 [8, 8192], P(None, 'dir'), may hold values from -3.140625 to 3.140625
- slot_parent: int32 [512], replicated, may hold values from 0 to 511, each once
- far_list: int32 [512, 189], replicated, may hold values from -1 to 511, as said below
- trans: float32 [2, 343, 8192], P(None, None, 'dir'), may hold values from -0.15625 to 0.15625
Outputs:
- far_field: float32 [512, 2, 8, 8192], P('box', None, None, 'dir')
The draws below stay inside these ranges and needn't reach their ends.
Inputs may be any that keep to these rules, and one draw needn't show every extreme that they name: `interp_blocks`: entry (j, b) is (j * 16 // 64 + o) modulo 16, for four different o of -2 to 2 in increasing order. `far_list`: row p lists, in increasing order of code(p, q), the occupied parents q whose own parents are neighbours of p's parent (coordinates differ by at most one) and that are not neighbours of p, then -1 to the end; each coordinate of q - p lies within -3 to 3; some row lists 189 partners.
All inputs are finite; a program needn't handle non-finite values.
Results may differ from the reference program's by a relative error of at most 0.0029.
Values may be sent and summed in bfloat16 or wider, within the bound.
No kernel may reach another device: no remote copies, remote signals or barrier semaphores. Data moves between devices by JAX's collectives and lax.ppermute only.
A program may use at most 384 MiB of HBM per device.

```python
import jax
import jax.numpy as jnp
from jax import lax

G = 8
PARENTS = 512
CHILD = 4096
K1 = 2048
K2 = 8192
BS = 128
NB = 4
NBI = 16
NBO = 64
FAR = 189
OFFS = 343
R = 8


def draw_interp_blocks(key, part):
    drop = jax.random.randint(jax.random.fold_in(key, 7), (NBO, 1), 0, 5)
    steps = jnp.arange(NB, dtype=jnp.int32)[None, :]
    offset = jnp.where(steps >= drop, steps + 1, steps) - 2
    center = (jnp.arange(NBO, dtype=jnp.int32) * NBI // NBO)[:, None]
    return ((center + offset) % NBI).astype(jnp.int32)


def draw_far_list(key, part):
    ident = jnp.arange(PARENTS, dtype=jnp.int32)
    pos_x = ident // (G * G)
    pos_y = ident // G % G
    pos_z = ident % G
    center = jax.random.randint(jax.random.fold_in(key, 12), (3,), 1, G // 2 - 1)
    lower = 2 * center - 2
    upper = 2 * center + 3
    inside = (pos_x >= lower[0]) & (pos_x <= upper[0]) & (pos_y >= lower[1]) & (pos_y <= upper[1]) & (pos_z >= lower[2]) & (pos_z <= upper[2])
    filled = (jax.random.randint(jax.random.fold_in(key, 11), (PARENTS,), 0, 10) < 7) | inside
    codes = jnp.arange(343, dtype=jnp.int32)
    off_x = codes // 49 - 3
    off_y = codes // 7 % 7 - 3
    off_z = codes % 7 - 3
    tgt_x = pos_x[:, None] + off_x[None, :]
    tgt_y = pos_y[:, None] + off_y[None, :]
    tgt_z = pos_z[:, None] + off_z[None, :]
    in_grid = (tgt_x >= 0) & (tgt_x < G) & (tgt_y >= 0) & (tgt_y < G) & (tgt_z >= 0) & (tgt_z < G)
    grand_ok = (jnp.abs(tgt_x // 2 - pos_x[:, None] // 2) <= 1) & (jnp.abs(tgt_y // 2 - pos_y[:, None] // 2) <= 1) & (jnp.abs(tgt_z // 2 - pos_z[:, None] // 2) <= 1)
    reach = jnp.maximum(jnp.maximum(jnp.abs(off_x), jnp.abs(off_y)), jnp.abs(off_z))
    not_near = (reach >= 2)[None, :]
    target = jnp.where(in_grid, tgt_x * G * G + tgt_y * G + tgt_z, 0)
    valid = in_grid & grand_ok & not_near & filled[target]
    sort_key = jnp.where(valid, codes[None, :], 343 + codes[None, :])
    order = jnp.argsort(sort_key, axis=1)[:, :FAR]
    chosen_valid = jnp.take_along_axis(valid, order, axis=1)
    chosen = jnp.take_along_axis(target, order, axis=1)
    return jnp.where(chosen_valid, chosen, -1).astype(jnp.int32)


def levels(stream_key, shape, cuts, smallest, largest):
    level, own = 1.0, jax.random.fold_in(stream_key, 6)
    for dim, shards_of in cuts:
        steps = jnp.exp(jax.random.uniform(jax.random.fold_in(own, dim), (shards_of,), jnp.float32, smallest / len(cuts), largest / len(cuts)))
        level = level * jnp.repeat(steps, shape[dim] // shards_of).reshape([-1 if axis == dim else 1 for axis in range(len(shape))])
    return level


def normal_values(own_key, shape, spread, most, pieces=(), kind=jnp.bfloat16):
    loudness = levels(own_key, shape, pieces, -0.22, 0.18) if pieces else 1.0
    entries = jax.random.normal(own_key, shape, jnp.float32) * spread * loudness
    return jnp.minimum(jnp.maximum(entries, -most), most).astype(kind)


def setup_inputs(seed: int = 0) -> dict:
    streams_of = jax.random.split(jax.random.key(seed), 8)
    child_pat = normal_values(streams_of[0], (CHILD, 2, R, K1), 1.0, 6.0, ((0, 8), (3, 4)))
    interp = normal_values(streams_of[1], (NBO, NB, BS, BS), (NB * BS) ** -0.5, 0.25, ((0, 4),))
    interp_blocks = draw_interp_blocks(jax.random.fold_in(streams_of[7], 71), 0)
    shift_angle = jnp.clip(jax.random.uniform(streams_of[3], (8, K2), jnp.float32, -3.140625, 3.140625), -3.140625, 3.140625)
    slot_parent = jax.random.permutation(streams_of[4], PARENTS).astype(jnp.int32)
    far_list = draw_far_list(jax.random.fold_in(streams_of[7], 71), 0)
    trans = normal_values(streams_of[6], (2, OFFS, K2), (8 * FAR) ** -0.5, 0.15625, ((2, 4),), jnp.float32)
    return dict(child_pat=child_pat, interp=interp, interp_blocks=interp_blocks, shift_angle=shift_angle, slot_parent=slot_parent, far_list=far_list, trans=trans)


def translate(patterns, table, slot_parent, slot_of, far_list, targets):
    parent = slot_parent[targets]
    listed = far_list[parent]
    valid = listed >= 0
    partner = jnp.where(valid, listed, 0)
    source = slot_of[partner]
    pos_x = (parent // (G * G))[:, None]
    pos_y = ((parent // G) % G)[:, None]
    pos_z = (parent % G)[:, None]
    code = (partner // (G * G) - pos_x + 3) * 49 + ((partner // G) % G - pos_y + 3) * 7 + (partner % G - pos_z + 3)
    code = jnp.where(valid, code, 0)
    mask = valid.astype(jnp.float32)[:, :, None]
    real_tab = (table[0][code] * mask)[:, :, None, :]
    imag_tab = (table[1][code] * mask)[:, :, None, :]
    rows = patterns[source].astype(jnp.float32)
    out_real = jnp.sum(real_tab * rows[:, :, 0] - imag_tab * rows[:, :, 1], axis=1)
    out_imag = jnp.sum(real_tab * rows[:, :, 1] + imag_tab * rows[:, :, 0], axis=1)
    return jnp.stack([out_real, out_imag], axis=1)


def reference(child_pat, interp, interp_blocks, shift_angle, slot_parent, far_list, trans):
    def one_block(index):
        blocks = interp_blocks[index]
        total = jnp.zeros((CHILD * 2 * R, BS), jnp.float32)
        for part in range(NB):
            start = (blocks[part] * BS).astype(jnp.int32)
            piece = lax.dynamic_slice_in_dim(child_pat, start, BS, 3).reshape(CHILD * 2 * R, BS)
            total = total + jnp.dot(piece, interp[index, part], preferred_element_type=jnp.float32)
        upsampled = total.reshape(PARENTS, 8, 2, R, BS)
        angle = lax.dynamic_slice_in_dim(shift_angle, (index * BS).astype(jnp.int32), BS, 1)
        cosine = jnp.cos(angle)[None, :, None, :]
        sine = jnp.sin(angle)[None, :, None, :]
        real_part = upsampled[:, :, 0]
        imag_part = upsampled[:, :, 1]
        out_real = jnp.sum(cosine * real_part - sine * imag_part, axis=1)
        out_imag = jnp.sum(sine * real_part + cosine * imag_part, axis=1)
        return jnp.stack([out_real, out_imag], axis=1).astype(jnp.bfloat16)

    blocks_out = lax.map(one_block, jnp.arange(NBO, dtype=jnp.int32))
    parent_pat = jnp.transpose(blocks_out, (1, 2, 3, 0, 4)).reshape(PARENTS, 2, R, K2)
    slot_of = jnp.zeros((PARENTS,), jnp.int32).at[slot_parent].set(jnp.arange(PARENTS, dtype=jnp.int32))

    def one_slot(target):
        return translate(parent_pat, trans, slot_parent, slot_of, far_list, target[None])[0]

    return lax.map(one_slot, jnp.arange(PARENTS, dtype=jnp.int32))
```

```python
import functools

import jax
import jax.numpy as jnp
import numpy as np
from jax import lax
from jax.experimental import pallas as pl
from jax.experimental.pallas import tpu as pltpu
from jax.sharding import PartitionSpec as P

LANES = 128
G = 8
HALF = G // 2
POINTS = 5
FREQ = 128
MIB = 1024 * 1024


def parent_order():
    octant = np.arange(8)
    grand = np.arange(HALF**3)
    ox, oy, oz = octant // 4, octant // 2 % 2, octant % 2
    gx, gy, gz = grand // HALF**2, grand // HALF % HALF, grand % HALF
    x = 2 * gx[None, :] + ox[:, None]
    y = 2 * gy[None, :] + oy[:, None]
    z = 2 * gz[None, :] + oz[:, None]
    return (x * G * G + y * G + z).reshape(-1).astype(np.int32)


def cover_rows():
    rows = []
    for low, high in ((3, 4), (2, 5)):
        for x in (low, high):
            for y in (low, high):
                for z in (low, high):
                    rows.append((x, y, z))
    seen = np.zeros((G, G, G), bool)
    axis = np.arange(G)
    for x, y, z in rows:
        near = [np.abs(axis - c) <= 1 for c in (x, y, z)]
        reach = [np.abs(axis // 2 - c // 2) <= 1 for c in (x, y, z)]
        cube = [v[0][:, None, None] & v[1][None, :, None] & v[2][None, None, :] for v in (near, reach)]
        seen |= cube[1] & ~cube[0]
    assert seen.all()
    return np.array([(x * G + y) * G + z for x, y, z in rows], np.int32)


def freq_points():
    index = np.arange(POINTS**3)
    return np.stack([index // POINTS**2, index // POINTS % POINTS, index % POINTS], 1)


def grid_points(side, start):
    index = np.arange(side**3)
    return np.stack([index // side**2, index // side % side, index % side], 1) + start


def real_form(matrix):
    return np.block([[matrix.real, -matrix.imag], [matrix.imag, matrix.real]])


def pad_rows(matrix, rows):
    return np.concatenate([matrix, np.zeros((rows - matrix.shape[0], matrix.shape[1]), matrix.dtype)])


def split(matrix):
    high = matrix.astype(jnp.bfloat16)
    low = (matrix - high.astype(np.float64)).astype(jnp.bfloat16)
    return high, low


def forward_matrix():
    phase = np.exp(-2j * np.pi / POINTS * (freq_points() @ grid_points(HALF, 0).T))
    high, low = split(real_form(pad_rows(phase, FREQ)))
    return np.concatenate([high, low], 1)


def inverse_matrix():
    phase = np.exp(2j * np.pi / POINTS * (grid_points(HALF, 0) @ freq_points().T)) / POINTS**3
    phase = pad_rows(phase.T, FREQ).T
    high, low = split(real_form(phase))
    return np.concatenate([high, high, low], 1)


def table_matrix():
    phase = np.exp(2j * np.pi / POINTS * (freq_points() @ grid_points(3, -1).T))
    return real_form(pad_rows(phase, FREQ)).astype(np.float32)


def tap_codes():
    delta = grid_points(3, -1)
    tap = grid_points(3, -1)
    offset = 2 * tap[None, :, :] + delta[:, None, :]
    code = ((offset + 3) * np.array([49, 7, 1])).sum(-1)
    far = np.abs(offset).max(-1) >= 2
    return code.astype(np.int32), far.astype(np.float32)


def table_of(trans, first, width, repeat):
    part = lax.dynamic_slice_in_dim(trans, first, width, 2)
    code, far = tap_codes()
    deltas, taps = code.shape
    rows = jnp.take(part, code.reshape(-1), axis=1).reshape(2, deltas, taps, width)
    rows = rows * far[None, :, :, None]
    matrix = jnp.asarray(table_matrix().reshape(2, FREQ, 2, taps))
    hat = jnp.einsum("cfet,edtk->cdfk", matrix, rows, precision=lax.Precision.HIGHEST)
    real, imag = hat[0], hat[1]
    forms = jnp.stack([real, imag - real, real + imag])
    return jnp.tile(forms, (1, 1, 1, repeat))


def upsample_kernel(offsets, me_ref, own, left, right, interp, cosine, sine, *rest, centers, tiles, roll):
    outs = rest[:tiles]
    weights, held = rest[tiles:]
    blocks_in = own.shape[1] // LANES
    per_center = weights.shape[2] // LANES
    window = weights.shape[1] // LANES
    half = window // 2
    slots = own.shape[0] // LANES
    left_blocks = left.shape[1] // LANES

    @pl.when(pl.program_id(0) == 0)
    def _():
        weights[...] = jnp.zeros_like(weights)
        for index, center in enumerate(centers):
            for j in range(per_center):
                row = center * per_center + j
                for b in range(interp.shape[1]):
                    start = pl.multiple_of(offsets[row, b] * LANES, LANES)
                    weights[index, pl.ds(start, LANES), j * LANES : (j + 1) * LANES] = interp[row, b]

    group = 4
    rows = group * LANES

    def step(i, carry):
        base = pl.multiple_of(i * rows, rows)
        for index, center in enumerate(centers):
            low, high = center - half, center + half + 1
            pieces = []
            if low < 0:
                pieces.append(left[pl.ds(base, rows), (left_blocks + low) * LANES :])
            pieces.append(own[pl.ds(base, rows), max(low, 0) * LANES : min(high, blocks_in) * LANES])
            if high > blocks_in:
                pieces.append(right[pl.ds(base, rows), : (high - blocks_in) * LANES])
            u = jnp.dot(
                jnp.concatenate(pieces, axis=1), weights[index], preferred_element_type=jnp.float32
            )
            u = u.reshape(group, 8, 2, 8, per_center * LANES)
            columns = slice(center * per_center * LANES, (center + 1) * per_center * LANES)
            real = jnp.zeros((group, 8, per_center * LANES), jnp.float32)
            imag = real
            for h in range(8):
                c = cosine[h : h + 1, columns][None]
                s = sine[h : h + 1, columns][None]
                real += c * u[:, h, 0] - s * u[:, h, 1]
                imag += s * u[:, h, 0] + c * u[:, h, 1]
            real = real.reshape(group * 8, per_center * LANES)
            imag = imag.reshape(group * 8, per_center * LANES)
            at = pl.ds(pl.multiple_of(i * group * 8, group * 8), group * 8)
            for j in range(per_center):
                lanes = slice(j * LANES, (j + 1) * LANES)
                held[index * per_center + j, 0, at, :] = real[:, lanes]
                held[index * per_center + j, 1, at, :] = imag[:, lanes]
        return carry

    lax.fori_loop(0, slots // group, step, 0)
    for s in range(tiles):
        tile = lax.rem(me_ref[0] + s, tiles) if roll else s
        for t in range(2):
            for r in range(8):
                outs[s][t, r] = held[tile, t, pl.ds(r, slots, stride=8), :].astype(jnp.bfloat16)


def upsample(own, left, right, interp, offsets, cosine, sine, me, centers, roll):
    rows = own.shape[0]
    slots = rows // LANES
    block = min(16, slots)
    per_center = interp.shape[0] // (own.shape[1] // LANES)
    window = 5
    tiles = len(centers) * per_center
    depth = block * LANES

    def rowwise(array):
        return pl.BlockSpec((depth, array.shape[1]), lambda i: (i, 0))

    whole = pl.BlockSpec(memory_space=pltpu.VMEM)
    smem = pl.BlockSpec(memory_space=pltpu.SMEM)
    return pl.pallas_call(
        functools.partial(upsample_kernel, centers=centers, tiles=tiles, roll=roll),
        grid=(slots // block,),
        in_specs=[smem, smem, rowwise(own), rowwise(left), rowwise(right), whole, whole, whole],
        out_specs=[pl.BlockSpec((2, 8, block, LANES), lambda i: (0, 0, i, 0))] * tiles,
        out_shape=[jax.ShapeDtypeStruct((2, 8, slots, LANES), jnp.bfloat16)] * tiles,
        scratch_shapes=[
            pltpu.VMEM((len(centers), window * LANES, per_center * LANES), jnp.bfloat16),
            pltpu.VMEM((tiles, 2, block * 8, LANES), jnp.float32),
        ],
        compiler_params=pltpu.CompilerParams(vmem_limit_bytes=48 * MIB),
        cost_estimate=pl.CostEstimate(
            flops=2 * rows * window * LANES * tiles * LANES, bytes_accessed=14 * MIB, transcendentals=0
        ),
        name="upsample",
    )(offsets, me, own, left, right, interp, cosine, sine)


def far_kernel(into, back, forward, inverse, table, *rest, count):
    ins = rest[:count]
    outs = rest[count : 2 * count]
    moved, hat, prod, near = rest[2 * count :]
    grand = HALF**3
    slots = ins[0].shape[2]

    for t in range(2):
        columns = [jnp.concatenate([ref[t, r] for ref in ins], axis=0) for r in range(2)]
        rows = jnp.concatenate(columns, axis=1)
        moved[t] = jnp.dot(into[...], rows, preferred_element_type=jnp.float32).astype(jnp.bfloat16)

    for octant in range(8):
        at = slice(octant * grand, (octant + 1) * grand)
        both = jnp.concatenate([moved[0, at], moved[1, at]], axis=0)
        both = jnp.concatenate([both, both], axis=0)
        hat[octant] = jnp.dot(forward[...], both, preferred_element_type=jnp.float32)

    def products(i, carry):
        at = pl.multiple_of(i * 8, 8)
        real_at, imag_at = pl.ds(at, 8), pl.ds(FREQ + at, 8)
        for r in range(2):
            lanes = slice(r * LANES, (r + 1) * LANES)
            real = [hat[s, real_at, lanes] for s in range(8)]
            imag = [hat[s, imag_at, lanes] for s in range(8)]
            total = [a + b for a, b in zip(real, imag)]
            for t in range(8):
                sums = [None] * 3
                for s in range(8):
                    delta = 0
                    for shift in (2, 1, 0):
                        delta = delta * 3 + (s >> shift & 1) - (t >> shift & 1) + 1
                    terms = (
                        table[0, delta, real_at] * total[s],
                        table[1, delta, real_at] * real[s],
                        table[2, delta, real_at] * imag[s],
                    )
                    sums = [b if a is None else a + b for a, b in zip(sums, terms)]
                prod[t, real_at, lanes] = sums[0] - sums[2]
                prod[t, imag_at, lanes] = sums[0] + sums[1]
        return carry

    lax.fori_loop(0, FREQ // 8, products, 0)

    for octant in range(8):
        value = prod[octant]
        high = value.astype(jnp.bfloat16)
        low = (value - high.astype(jnp.float32)).astype(jnp.bfloat16)
        stacked = jnp.concatenate([high, low, high], axis=0)
        result = jnp.dot(inverse[...], stacked, preferred_element_type=jnp.float32)
        at = slice(octant * grand, (octant + 1) * grand)
        near[0, at] = result[:grand].astype(jnp.bfloat16)
        near[1, at] = result[grand:].astype(jnp.bfloat16)

    for t in range(2):
        result = jnp.dot(back[...], near[t], preferred_element_type=jnp.float32).astype(jnp.bfloat16)
        for index, ref in enumerate(outs):
            for r in range(2):
                ref[t, r] = result[index * slots : (index + 1) * slots, r * LANES : (r + 1) * LANES]


def far_field(pieces, into, back, table):
    count = len(pieces)
    _, columns, slots, _ = pieces[0].shape
    parents = into.shape[0]
    whole = pl.BlockSpec(memory_space=pltpu.VMEM)
    piece = pl.BlockSpec((2, 2, slots, LANES), lambda i: (0, i, 0, 0))
    return pl.pallas_call(
        functools.partial(far_kernel, count=count),
        grid=(columns // 2,),
        in_specs=[whole] * 5 + [piece] * count,
        out_specs=[piece] * count,
        out_shape=[jax.ShapeDtypeStruct(pieces[0].shape, jnp.bfloat16)] * count,
        scratch_shapes=[
            pltpu.VMEM((2, parents, 2 * LANES), jnp.bfloat16),
            pltpu.VMEM((8, 2 * FREQ, 2 * LANES), jnp.float32),
            pltpu.VMEM((8, 2 * FREQ, 2 * LANES), jnp.float32),
            pltpu.VMEM((2, parents, 2 * LANES), jnp.bfloat16),
        ],
        compiler_params=pltpu.CompilerParams(vmem_limit_bytes=48 * MIB),
        cost_estimate=pl.CostEstimate(flops=10_000_000_000, bytes_accessed=12 * MIB, transcendentals=0),
        name="far_field",
    )(into, back, jnp.asarray(forward_matrix()), jnp.asarray(inverse_matrix()), table, *pieces)


def finish_kernel(me_ref, *refs, chunks, tiles, first_tile):
    ins = refs[: chunks * tiles]
    out, held = refs[chunks * tiles :]
    slots = ins[0].shape[2]
    for chunk in range(chunks):
        for s in range(tiles):
            tile = lax.rem(me_ref[0] + tiles - s, tiles)
            ref = ins[chunk * tiles + s]
            for t in range(2):
                for r in range(8):
                    held[tile, pl.ds(t * 8 + r, slots, stride=16), :] = ref[t, r].astype(jnp.float32)
        for tile in range(tiles):
            at = first_tile[chunk][tile] * LANES
            out[:, at : at + LANES] = held[tile]


def finish(results, me, first_tile):
    chunks, tiles = len(results), len(results[0])
    slots = results[0][0].shape[2]
    block = min(16, slots)
    width = chunks * tiles * LANES
    return pl.pallas_call(
        functools.partial(finish_kernel, chunks=chunks, tiles=tiles, first_tile=first_tile),
        grid=(slots // block,),
        in_specs=[pl.BlockSpec(memory_space=pltpu.SMEM)]
        + [pl.BlockSpec((2, 8, block, LANES), lambda i: (0, 0, i, 0))] * (chunks * tiles),
        out_specs=pl.BlockSpec((block * 16, width), lambda i: (i, 0)),
        out_shape=jax.ShapeDtypeStruct((slots * 16, width), jnp.float32),
        scratch_shapes=[pltpu.VMEM((tiles, block * 16, LANES), jnp.float32)],
        compiler_params=pltpu.CompilerParams(vmem_limit_bytes=48 * MIB),
        name="finish",
    )(me, *[piece for result in results for piece in result])


def exchange(pieces, axis):
    devices = len(pieces)
    moved = [pieces[0]]
    for s in range(1, devices):
        moved.append(lax.ppermute(pieces[s], axis, [(i, (i + s) % devices) for i in range(devices)]))
    return moved


def shards(child_pat, interp, interp_blocks, shift_angle, slot_parent, far_list, trans):
    boxes = lax.axis_size("box")
    box = lax.axis_index("box")
    directions = lax.axis_size("dir")
    children, _, columns, width_in = child_pat.shape
    local_in = width_in // LANES
    per_center = interp.shape[0] // local_in
    total_in = local_in * directions
    slots = children // 8
    rows = children * 2 * columns
    own = child_pat.reshape(rows, width_in)
    me = box.reshape(1).astype(jnp.int32)

    up = [(i, (i + 1) % directions) for i in range(directions)]
    down = [(j, i) for i, j in up]

    def block_of(index):
        return lax.slice_in_dim(own, index * LANES, (index + 1) * LANES, axis=1)

    before1 = lax.ppermute(block_of(local_in - 1), "dir", up)
    after0 = lax.ppermute(block_of(0), "dir", down)
    before0 = lax.ppermute(block_of(local_in - 2), "dir", up)
    after1 = lax.ppermute(block_of(1), "dir", down)

    centers = jnp.arange(interp.shape[0], dtype=jnp.int32) // per_center + lax.axis_index("dir") * local_in
    offsets = (interp_blocks - centers[:, None] + 2) % total_in
    cosine = jnp.cos(shift_angle)
    sine = jnp.sin(shift_angle)

    pairs = [(i, local_in - 1 - i) for i in reversed(range(local_in // 2))]
    tiles = 2 * per_center
    share = tiles * LANES // boxes
    repeat = max(1, LANES // share)
    assert share * repeat == LANES and columns % (2 * repeat) == 0

    order = parent_order()
    listed = jnp.concatenate([far_list[row] for row in cover_rows()])
    occupied = jnp.any(listed[:, None] == order[None, :], axis=0)
    parent_of = slot_parent.reshape(boxes, slots)
    shifts = jnp.arange(boxes, dtype=jnp.int32)
    arriving = parent_of[(box - shifts) % boxes].reshape(-1)
    leaving = parent_of[(box + shifts) % boxes].reshape(-1)
    into = ((arriving[None, :] == order[:, None]) & occupied[:, None]).astype(jnp.bfloat16)
    back = (leaving[:, None] == order[None, :]).astype(jnp.bfloat16)

    tables = []
    for low, high in pairs:
        at = box * share
        middle = per_center * LANES
        first = jnp.where(at < middle, low * middle + at, high * middle + at - middle)
        tables.append(table_of(trans, first, share, repeat))

    def pieces_of(values):
        if repeat == 1:
            return values
        value = jnp.stack(values).reshape(tiles, 2, columns // repeat, repeat, slots, repeat, share)
        value = value.transpose(0, 5, 1, 2, 4, 3, 6).reshape(boxes, 2, columns // repeat, slots, LANES)
        value = jnp.roll(value, -box, axis=0)
        return [value[s] for s in range(boxes)]

    def tiles_of(values):
        value = jnp.roll(jnp.stack(values)[::-1], box + 1, axis=0)
        value = value.reshape(tiles, repeat, 2, columns // repeat, slots, repeat, share)
        value = value.transpose(4, 2, 3, 5, 0, 1, 6).reshape(slots, 2, columns, 2, per_center * LANES)
        return value.astype(jnp.float32)

    sides = [(before1, after0)]
    sides.append((jnp.concatenate([before0, before1], axis=1), jnp.concatenate([after0, after1], axis=1)))
    results = []
    for index, pair in enumerate(pairs):
        left, right = sides[index]
        patterns = upsample(own, left, right, interp, offsets, cosine, sine, me, pair, repeat == 1)
        gathered = exchange(pieces_of(patterns), "box")
        results.append(gathered)
    results = [far_field(gathered, into, back, table) for gathered, table in zip(results, tables)]
    results = [exchange(result, "box") for result in results]

    if repeat == 1:
        first_tile = [[pair[t // per_center] * per_center + t % per_center for t in range(tiles)] for pair in pairs]
        out = finish(results, me, first_tile)
        return out.reshape(slots, 2, columns, local_in * per_center * LANES)
    parts = [None] * local_in
    for pair, result in zip(pairs, results):
        value = tiles_of(result)
        for side, center in enumerate(pair):
            parts[center] = value[:, :, :, side]
    return jnp.concatenate(parts, axis=-1)


def solution(mesh):
    in_specs = (
        P("box", None, None, "dir"),
        P("dir", None, None, None),
        P("dir", None),
        P(None, "dir"),
        P(),
        P(),
        P(None, None, "dir"),
    )
    out_specs = P("box", None, None, "dir")
    return jax.shard_map(shards, mesh=mesh, in_specs=in_specs, out_specs=out_specs, check_vma=False)
```

```python
import functools

import jax
import jax.numpy as jnp
import numpy as np
from jax import lax
from jax.experimental import pallas as pl
from jax.experimental.pallas import tpu as pltpu
from jax.sharding import PartitionSpec as P

LANES = 128
G = 8
HALF = G // 2
POINTS = 5
FREQ = 128
MIB = 1024 * 1024


def parent_order():
    octant = np.arange(8)
    grand = np.arange(HALF**3)
    ox, oy, oz = octant // 4, octant // 2 % 2, octant % 2
    gx, gy, gz = grand // HALF**2, grand // HALF % HALF, grand % HALF
    x = 2 * gx[None, :] + ox[:, None]
    y = 2 * gy[None, :] + oy[:, None]
    z = 2 * gz[None, :] + oz[:, None]
    return (x * G * G + y * G + z).reshape(-1).astype(np.int32)


def cover_rows():
    rows = []
    for low, high in ((3, 4), (2, 5)):
        for x in (low, high):
            for y in (low, high):
                for z in (low, high):
                    rows.append((x, y, z))
    seen = np.zeros((G, G, G), bool)
    axis = np.arange(G)
    for x, y, z in rows:
        near = [np.abs(axis - c) <= 1 for c in (x, y, z)]
        reach = [np.abs(axis // 2 - c // 2) <= 1 for c in (x, y, z)]
        cube = [v[0][:, None, None] & v[1][None, :, None] & v[2][None, None, :] for v in (near, reach)]
        seen |= cube[1] & ~cube[0]
    assert seen.all()
    return np.array([(x * G + y) * G + z for x, y, z in rows], np.int32)


def freq_points():
    index = np.arange(POINTS**3)
    return np.stack([index // POINTS**2, index // POINTS % POINTS, index % POINTS], 1)


def grid_points(side, start):
    index = np.arange(side**3)
    return np.stack([index // side**2, index // side % side, index % side], 1) + start


def real_form(matrix):
    return np.block([[matrix.real, -matrix.imag], [matrix.imag, matrix.real]])


def pad_rows(matrix, rows):
    return np.concatenate([matrix, np.zeros((rows - matrix.shape[0], matrix.shape[1]), matrix.dtype)])


def split(matrix):
    high = matrix.astype(jnp.bfloat16)
    low = (matrix - high.astype(np.float64)).astype(jnp.bfloat16)
    return high, low


def forward_matrix():
    phase = np.exp(-2j * np.pi / POINTS * (freq_points() @ grid_points(HALF, 0).T))
    high, low = split(real_form(pad_rows(phase, FREQ)))
    return np.concatenate([high, low], 1)


def inverse_matrix():
    phase = np.exp(2j * np.pi / POINTS * (grid_points(HALF, 0) @ freq_points().T)) / POINTS**3
    phase = pad_rows(phase.T, FREQ).T
    high, low = split(real_form(phase))
    return np.concatenate([high, high, low], 1)


TAP_ROWS = 40


def table_matrix():
    phase = np.exp(2j * np.pi / POINTS * (freq_points() @ grid_points(3, -1).T))
    phase = np.concatenate([phase.reshape(-1, 9, 3), np.zeros((POINTS**3, 9, 1))], 2).reshape(-1, 36)
    phase = pad_rows(pad_rows(phase, FREQ).T, TAP_ROWS).T
    high, low = split(real_form(phase))
    return np.concatenate([high, high, low], 1)


def far_codes():
    return (np.abs(grid_points(7, -3)).max(1) >= 2).astype(np.float32)


def table_kernel(place, matrix, far, operator, out, kept, taps):
    codes = operator.shape[0]
    kept[...] = jnp.zeros_like(kept)
    taps[...] = jnp.zeros_like(taps)
    for half in range(2):
        kept[half, :codes] = operator[:, half, :] * far[...]
    for delta, (x, y, z) in enumerate(grid_points(3, 0)):
        for half in range(2):
            for tap in range(9):
                code = (x + 2 * (tap // 3)) * 49 + (y + 2 * (tap % 3)) * 7 + z
                taps[half, 4 * tap : 4 * tap + 4] = kept[half, pl.ds(int(code), 4, stride=2), :]
        value = jnp.concatenate([taps[0], taps[1]], axis=0)
        high = value.astype(jnp.bfloat16)
        low = (value - high.astype(jnp.float32)).astype(jnp.bfloat16)
        stacked = jnp.concatenate([high, low, high], axis=0)
        result = jnp.dot(matrix[...], stacked, preferred_element_type=jnp.float32)
        real, imag = result[:FREQ], result[FREQ:]
        out[0, delta] = real
        out[1, delta] = imag - real
        out[2, delta] = real + imag


def table_of(trans, first, width, repeat):
    trans = jnp.swapaxes(trans, 0, 1)
    codes = trans.shape[0]
    if repeat > 1:
        trans = jnp.tile(lax.dynamic_slice_in_dim(trans, first, width, 2), (1, 1, repeat))
        first = jnp.zeros_like(first)
    whole = pl.BlockSpec(memory_space=pltpu.VMEM)
    return pl.pallas_call(
        table_kernel,
        grid_spec=pltpu.PrefetchScalarGridSpec(
            num_scalar_prefetch=1,
            grid=(1,),
            in_specs=[whole, whole, pl.BlockSpec((codes, 2, LANES), lambda i, place: (0, 0, place[0]))],
            out_specs=pl.BlockSpec((3, 27, FREQ, LANES), lambda i, place: (0, 0, 0, 0)),
            scratch_shapes=[
                pltpu.VMEM((2, (codes // 8 + 2) * 8, LANES), jnp.float32),
                pltpu.VMEM((2, TAP_ROWS, LANES), jnp.float32),
            ],
        ),
        out_shape=jax.ShapeDtypeStruct((3, 27, FREQ, LANES), jnp.float32),
        compiler_params=pltpu.CompilerParams(vmem_limit_bytes=32 * MIB),
        cost_estimate=pl.CostEstimate(flops=1_000_000_000, bytes_accessed=MIB, transcendentals=0),
        name="table",
    )((first // LANES).reshape(1), jnp.asarray(table_matrix()), jnp.asarray(far_codes())[:, None], trans)


def upsample_kernel(places, first, own, halo, interp, cosine, sine, out, weights, held):
    tiles = out.shape[0]
    slots = own.shape[0] // LANES
    lanes = 2 * LANES

    @pl.when(pl.program_id(0) == 0)
    def _():
        weights[...] = jnp.zeros_like(weights)
        for j in range(tiles):
            for b in range(interp.shape[1]):
                start = pl.multiple_of(places[j, b] * LANES, LANES)
                weights[pl.ds(start, LANES), j * LANES : (j + 1) * LANES] = interp[first[0] + j, b]

    group = 4
    rows = group * LANES
    for i in range(slots // group):
        at = slice(i * rows, (i + 1) * rows)
        value = jnp.concatenate([own[at, :], halo[at, :]], axis=1)
        for n in range(tiles // 2):
            columns = slice(n * lanes, (n + 1) * lanes)
            u = jnp.dot(value, weights[:, columns], preferred_element_type=jnp.float32)
            u = u.reshape(group, 8, 2, 8, lanes)
            real = imag = None
            for h in range(8):
                c = cosine[h : h + 1, columns][None]
                s = sine[h : h + 1, columns][None]
                x = c * u[:, h, 0] - s * u[:, h, 1]
                y = s * u[:, h, 0] + c * u[:, h, 1]
                real, imag = (x, y) if h == 0 else (real + x, imag + y)
            kept = slice(i * group * 8, (i + 1) * group * 8)
            for t, part in enumerate((real, imag)):
                part = part.reshape(group * 8, lanes)
                held[2 * n, t, kept, :] = part[:, :LANES]
                held[2 * n + 1, t, kept, :] = part[:, LANES:]
    for tile in range(tiles):
        for t in range(2):
            for r in range(8):
                out[tile, t, r] = held[tile, t, pl.ds(r, slots, stride=8), :].astype(jnp.bfloat16)


def upsample(own, halo, interp, places, first, cosine, sine, begin, cost):
    rows = halo.shape[0]
    slots = rows // LANES
    block = min(16, slots)
    steps = slots // block
    tiles = places.shape[0]
    depth = block * LANES
    width = own.shape[1] + halo.shape[1]
    whole = pl.BlockSpec(memory_space=pltpu.VMEM)
    smem = pl.BlockSpec(memory_space=pltpu.SMEM)
    return pl.pallas_call(
        upsample_kernel,
        grid=(steps,),
        in_specs=[
            smem,
            smem,
            pl.BlockSpec((depth, own.shape[1]), lambda i: (begin // block + i, 0)),
            pl.BlockSpec((depth, halo.shape[1]), lambda i: (i, 0)),
            whole,
            whole,
            whole,
        ],
        out_specs=pl.BlockSpec((tiles, 2, 8, block, LANES), lambda i: (0, 0, 0, i, 0)),
        out_shape=jax.ShapeDtypeStruct((tiles, 2, 8, slots, LANES), jnp.bfloat16),
        scratch_shapes=[
            pltpu.VMEM((width, tiles * LANES), jnp.bfloat16),
            pltpu.VMEM((tiles, 2, block * 8, LANES), jnp.float32),
        ],
        compiler_params=pltpu.CompilerParams(vmem_limit_bytes=48 * MIB),
        cost_estimate=pl.CostEstimate(flops=cost, bytes_accessed=rows, transcendentals=0),
        name="upsample",
    )(places, first, own, halo, interp, cosine, sine)


def far_kernel(into, back, forward, inverse, table, *rest, count):
    ins = rest[:count]
    outs = rest[count:-4]
    moved, hat, prod, near = rest[-4:]
    grand = HALF**3
    boxes = ins[0].shape[0]
    slots = outs[0].shape[3]

    for t in range(2):
        columns = [
            jnp.concatenate([ref[box, t, r] for box in range(boxes) for ref in ins], axis=0) for r in range(2)
        ]
        rows = jnp.concatenate(columns, axis=1)
        moved[t] = jnp.dot(into[...], rows, preferred_element_type=jnp.float32).astype(jnp.bfloat16)

    for octant in range(8):
        at = slice(octant * grand, (octant + 1) * grand)
        both = jnp.concatenate([moved[0, at], moved[1, at]], axis=0)
        both = jnp.concatenate([both, both], axis=0)
        hat[octant] = jnp.dot(forward[...], both, preferred_element_type=jnp.float32)

    def products(i, carry):
        at = pl.multiple_of(i * 8, 8)
        real_at, imag_at = pl.ds(at, 8), pl.ds(FREQ + at, 8)
        for r in range(2):
            lanes = slice(r * LANES, (r + 1) * LANES)
            real = [hat[s, real_at, lanes] for s in range(8)]
            imag = [hat[s, imag_at, lanes] for s in range(8)]
            total = [a + b for a, b in zip(real, imag)]
            for t in range(8):
                sums = [None] * 3
                for s in range(8):
                    delta = 0
                    for shift in (2, 1, 0):
                        delta = delta * 3 + (s >> shift & 1) - (t >> shift & 1) + 1
                    terms = (
                        table[0, delta, real_at] * total[s],
                        table[1, delta, real_at] * real[s],
                        table[2, delta, real_at] * imag[s],
                    )
                    sums = [b if a is None else a + b for a, b in zip(sums, terms)]
                prod[t, real_at, lanes] = sums[0] - sums[2]
                prod[t, imag_at, lanes] = sums[0] + sums[1]
        return carry

    lax.fori_loop(0, FREQ // 8, products, 0)

    for octant in range(8):
        value = prod[octant]
        high = value.astype(jnp.bfloat16)
        low = (value - high.astype(jnp.float32)).astype(jnp.bfloat16)
        stacked = jnp.concatenate([high, low, high], axis=0)
        result = jnp.dot(inverse[...], stacked, preferred_element_type=jnp.float32)
        at = slice(octant * grand, (octant + 1) * grand)
        near[0, at] = result[:grand].astype(jnp.bfloat16)
        near[1, at] = result[grand:].astype(jnp.bfloat16)

    for t in range(2):
        result = jnp.dot(back[...], near[t], preferred_element_type=jnp.float32).astype(jnp.bfloat16)
        for box in range(boxes):
            ref, index = (outs[box], 0) if len(outs) > 1 else (outs[0], box)
            for r in range(2):
                ref[index, t, r] = result[box * slots : (box + 1) * slots, r * LANES : (r + 1) * LANES]


def far_field(parts, into, back, table, apart):
    boxes, _, columns, _, _ = parts[0].shape
    slots = sum(part.shape[3] for part in parts)
    parents = into.shape[0]
    whole = pl.BlockSpec(memory_space=pltpu.VMEM)

    def columnwise(boxes, rows):
        return pl.BlockSpec((boxes, 2, 2, rows, LANES), lambda i: (0, 0, i, 0, 0))

    results, each = (boxes, 1) if apart else (1, boxes)
    return pl.pallas_call(
        functools.partial(far_kernel, count=len(parts)),
        grid=(columns // 2,),
        in_specs=[whole] * 5 + [columnwise(boxes, part.shape[3]) for part in parts],
        out_specs=[columnwise(each, slots)] * results,
        out_shape=[jax.ShapeDtypeStruct((each, 2, columns, slots, LANES), jnp.bfloat16)] * results,
        scratch_shapes=[
            pltpu.VMEM((2, parents, 2 * LANES), jnp.bfloat16),
            pltpu.VMEM((8, 2 * FREQ, 2 * LANES), jnp.float32),
            pltpu.VMEM((8, 2 * FREQ, 2 * LANES), jnp.float32),
            pltpu.VMEM((2, parents, 2 * LANES), jnp.bfloat16),
        ],
        compiler_params=pltpu.CompilerParams(vmem_limit_bytes=48 * MIB),
        cost_estimate=pl.CostEstimate(flops=20_000_000_000, bytes_accessed=12 * MIB, transcendentals=0),
        name="far_field",
    )(into, back, jnp.asarray(forward_matrix()), jnp.asarray(inverse_matrix()), table, *parts)


def finish_kernel(side, me, *rest, tiles):
    ins = rest[:tiles]
    out, held = rest[-2:]
    slots = ins[0].shape[3]
    for s in range(tiles):
        tile = lax.rem(me[0] + tiles - s, tiles)
        for t in range(2):
            for r in range(8):
                held[tile, pl.ds(t * 8 + r, slots, stride=16), :] = ins[s][0, t, r].astype(jnp.float32)
    for tile in range(tiles):
        out[:, tile * LANES : (tile + 1) * LANES] = held[tile]


def finish(results, whole, side, me, width):
    tiles = len(results)
    _, _, _, slots, _ = results[0].shape
    block = min(16, slots)
    kept = [] if whole is None else [whole]
    return pl.pallas_call(
        functools.partial(finish_kernel, tiles=tiles),
        grid_spec=pltpu.PrefetchScalarGridSpec(
            num_scalar_prefetch=2,
            grid=(slots // block,),
            in_specs=[pl.BlockSpec((1, 2, 8, block, LANES), lambda i, *_: (0, 0, 0, i, 0))] * tiles
            + [pl.BlockSpec(memory_space=pl.ANY)] * len(kept),
            out_specs=pl.BlockSpec((block * 16, tiles * LANES), lambda i, side, me: (i, side[0])),
            scratch_shapes=[pltpu.VMEM((tiles, block * 16, LANES), jnp.float32)],
        ),
        out_shape=jax.ShapeDtypeStruct((slots * 16, width), jnp.float32),
        input_output_aliases={2 + tiles: 0} if kept else {},
        compiler_params=pltpu.CompilerParams(vmem_limit_bytes=48 * MIB),
        name="finish",
    )(side, me, *results, *kept)


def exchange(value):
    return lax.all_to_all(value, "box", 0, 0, tiled=True)


def send_apart(pieces):
    devices = len(pieces)
    moved = list(pieces)
    for s in sorted(range(1, devices), key=lambda s: abs(s - devices // 2)):
        moved[s] = lax.ppermute(pieces[s], "box", [(i, (i + s) % devices) for i in range(devices)])
    return moved


def after(value, *others):
    return lax.optimization_barrier((value, *others))[0]


def shards(child_pat, interp, interp_blocks, shift_angle, slot_parent, far_list, trans):
    boxes = lax.axis_size("box")
    box = lax.axis_index("box").astype(jnp.int32)
    directions = lax.axis_size("dir")
    here = lax.axis_index("dir").astype(jnp.int32)
    children, _, columns, width_in = child_pat.shape
    local_in = width_in // LANES
    per_center = interp.shape[0] // local_in
    total_in = local_in * directions
    slots = children // 8
    rows = children * 2 * columns
    own = child_pat.reshape(rows, width_in)
    edge = 2 * LANES

    tiles = interp.shape[0] // 2
    width = tiles * LANES
    share = width // boxes
    repeat = max(1, LANES // share)
    apart = repeat == 1
    assert local_in == 4 and directions % 2 == 0
    assert share * repeat == LANES and columns % (2 * repeat) == 0

    odd = here % 2
    inner = [(i, i + 1 - 2 * (i % 2)) for i in range(directions)]
    outer = [(i, (i + 2 * (i % 2) - 1) % directions) for i in range(directions)]
    sides = [1 - odd, odd]
    def send_edge(source, step, begin, size):
        start = (begin * LANES, sides[step] * (width_in - edge))
        send = lax.dynamic_slice(source, start, (size * LANES, edge))
        return send, lax.ppermute(send, "dir", (inner, outer)[step])

    half = slots // 2
    quarter = half // 2
    send, inner_halo = send_edge(own, 0, 0, slots)
    _, outer_first = send_edge(after(own, send), 1, 0, quarter)

    centers = jnp.arange(interp.shape[0], dtype=jnp.int32) // per_center
    window = (interp_blocks - (centers + here * local_in)[:, None] + 2) % total_in + centers[:, None] - 2

    def places_for(side):
        block = lax.dynamic_slice_in_dim(window, side * tiles, tiles, 0)
        return jnp.where(block < 0, block + local_in + 2, block)

    def pieces_of(value):
        if apart:
            return value
        slots = value.shape[3]
        value = value.reshape(tiles, 2, columns // repeat, repeat, slots, repeat, share)
        return value.transpose(0, 5, 1, 2, 4, 3, 6).reshape(boxes, 2, columns // repeat, slots, LANES)

    def tiles_of(value):
        value = value.reshape(tiles, repeat, 2, columns // repeat, slots, repeat, share)
        return value.transpose(4, 2, 3, 5, 0, 1, 6).reshape(slots, 2, columns, width).astype(jnp.float32)

    def patterns(step, halo, begin, cost):
        angle = lax.dynamic_slice_in_dim(shift_angle, sides[step] * width, width, 1)
        first = (sides[step] * tiles).reshape(1)
        cosine, sine = jnp.cos(angle), jnp.sin(angle)
        return upsample(own, halo, interp, places_for(sides[step]), first, cosine, sine, begin, cost)

    def give_back(pieces):
        return send_apart(pieces) if apart else [exchange(pieces[0])]

    value = patterns(0, inner_halo, 0, 1)
    value, outer_first = lax.optimization_barrier((value, outer_first))
    first = exchange(pieces_of(value))
    _, outer_second = send_edge(after(own, value), 1, quarter, half - quarter)

    operator, slot_parent, far_list, _ = lax.optimization_barrier((trans, slot_parent, far_list, value))
    tables = [table_of(operator, side * width + box * share, share, repeat) for side in sides]
    order = parent_order()
    listed = jnp.concatenate([far_list[row] for row in cover_rows()])
    occupied = jnp.any(listed[:, None] == order[None, :], axis=0)
    into = ((slot_parent[None, :] == order[:, None]) & occupied[:, None]).astype(jnp.bfloat16)
    leaving = slot_parent.reshape(boxes, slots)
    if apart:
        leaving = leaving[(box + jnp.arange(boxes, dtype=jnp.int32)) % boxes]
    back = (leaving.reshape(-1)[:, None] == order[None, :]).astype(jnp.bfloat16)

    _, outer_last = send_edge(after(own, *tables), 1, half, slots - half)
    halo = jnp.concatenate([outer_first, outer_second], axis=0)
    value = patterns(1, after(halo, into, back, *tables), 0, 12_000_000_000)
    second = exchange(pieces_of(value))
    pieces = far_field([after(first, value)], into, back, tables[0], apart)
    value = patterns(1, after(outer_last, pieces[0], second), half, 12_000_000_000)
    third = exchange(pieces_of(value))
    pieces = [after(piece, third) for piece in pieces]
    results = [give_back(pieces)]
    pieces = far_field([second, third], into, back, tables[1], apart)
    results.append(give_back(pieces))

    out = None
    if apart:
        for result, side in zip(results, sides):
            out = finish(result, out, side.reshape(1), box.reshape(1), 2 * width)
        return out.reshape(slots, 2, columns, 2 * width)
    first, second = (tiles_of(result[0]) for result in results)
    ordered = [jnp.where(odd == 1, first, second), jnp.where(odd == 1, second, first)]
    return jnp.concatenate(ordered, axis=-1)


def solution(mesh):
    in_specs = (
        P("box", None, None, "dir"),
        P("dir", None, None, None),
        P("dir", None),
        P(None, "dir"),
        P(),
        P(),
        P(None, None, "dir"),
    )
    out_specs = P("box", None, None, "dir")
    return jax.shard_map(shards, mesh=mesh, in_specs=in_specs, out_specs=out_specs, check_vma=False)
```

```python
import functools

import jax
import jax.numpy as jnp
import numpy as np
from jax import lax
from jax.experimental import pallas as pl
from jax.experimental.pallas import tpu as pltpu
from jax.sharding import PartitionSpec as P

LANES = 128
G = 8
HALF = G // 2
POINTS = 5
FREQ = 128
MIB = 1024 * 1024


def parent_order():
    octant = np.arange(8)
    grand = np.arange(HALF**3)
    ox, oy, oz = octant // 4, octant // 2 % 2, octant % 2
    gx, gy, gz = grand // HALF**2, grand // HALF % HALF, grand % HALF
    x = 2 * gx[None, :] + ox[:, None]
    y = 2 * gy[None, :] + oy[:, None]
    z = 2 * gz[None, :] + oz[:, None]
    return (x * G * G + y * G + z).reshape(-1).astype(np.int32)


def cover_rows():
    rows = []
    for low, high in ((3, 4), (2, 5)):
        for x in (low, high):
            for y in (low, high):
                for z in (low, high):
                    rows.append((x, y, z))
    seen = np.zeros((G, G, G), bool)
    axis = np.arange(G)
    for x, y, z in rows:
        near = [np.abs(axis - c) <= 1 for c in (x, y, z)]
        reach = [np.abs(axis // 2 - c // 2) <= 1 for c in (x, y, z)]
        cube = [v[0][:, None, None] & v[1][None, :, None] & v[2][None, None, :] for v in (near, reach)]
        seen |= cube[1] & ~cube[0]
    assert seen.all()
    return np.array([(x * G + y) * G + z for x, y, z in rows], np.int32)


def freq_points():
    index = np.arange(POINTS**3)
    return np.stack([index // POINTS**2, index // POINTS % POINTS, index % POINTS], 1)


def grid_points(side, start):
    index = np.arange(side**3)
    return np.stack([index // side**2, index // side % side, index % side], 1) + start


def real_form(matrix):
    return np.block([[matrix.real, -matrix.imag], [matrix.imag, matrix.real]])


def pad_rows(matrix, rows):
    return np.concatenate([matrix, np.zeros((rows - matrix.shape[0], matrix.shape[1]), matrix.dtype)])


def split(matrix):
    high = matrix.astype(jnp.bfloat16)
    low = (matrix - high.astype(np.float64)).astype(jnp.bfloat16)
    return high, low


def forward_matrix():
    phase = np.exp(-2j * np.pi / POINTS * (freq_points() @ grid_points(HALF, 0).T))
    high, low = split(real_form(pad_rows(phase, FREQ)))
    return np.concatenate([high, low], 1)


def inverse_matrix():
    phase = np.exp(2j * np.pi / POINTS * (grid_points(HALF, 0) @ freq_points().T)) / POINTS**3
    phase = pad_rows(phase.T, FREQ).T
    high, low = split(real_form(phase))
    return np.concatenate([high, high, low], 1)


TAP_ROWS = 40


def table_matrix():
    phase = np.exp(2j * np.pi / POINTS * (freq_points() @ grid_points(3, -1).T))
    phase = np.concatenate([phase.reshape(-1, 9, 3), np.zeros((POINTS**3, 9, 1))], 2).reshape(-1, 36)
    phase = pad_rows(pad_rows(phase, FREQ).T, TAP_ROWS).T
    high, low = split(real_form(phase))
    return np.concatenate([high, high, low], 1)


def far_codes():
    return (np.abs(grid_points(7, -3)).max(1) >= 2).astype(np.float32)


def table_kernel(place, matrix, far, operator, out, kept, taps):
    codes = operator.shape[0]
    kept[...] = jnp.zeros_like(kept)
    taps[...] = jnp.zeros_like(taps)
    for half in range(2):
        kept[half, :codes] = operator[:, half, :] * far[...]
    for delta, (x, y, z) in enumerate(grid_points(3, 0)):
        for half in range(2):
            for tap in range(9):
                code = (x + 2 * (tap // 3)) * 49 + (y + 2 * (tap % 3)) * 7 + z
                taps[half, 4 * tap : 4 * tap + 4] = kept[half, pl.ds(int(code), 4, stride=2), :]
        value = jnp.concatenate([taps[0], taps[1]], axis=0)
        high = value.astype(jnp.bfloat16)
        low = (value - high.astype(jnp.float32)).astype(jnp.bfloat16)
        stacked = jnp.concatenate([high, low, high], axis=0)
        result = jnp.dot(matrix[...], stacked, preferred_element_type=jnp.float32)
        real, imag = result[:FREQ], result[FREQ:]
        out[0, delta] = real
        out[1, delta] = imag - real
        out[2, delta] = real + imag


def table_of(trans, first, width, repeat):
    trans = jnp.swapaxes(trans, 0, 1)
    codes = trans.shape[0]
    if repeat > 1:
        trans = jnp.tile(lax.dynamic_slice_in_dim(trans, first, width, 2), (1, 1, repeat))
        first = jnp.zeros_like(first)
    whole = pl.BlockSpec(memory_space=pltpu.VMEM)
    return pl.pallas_call(
        table_kernel,
        grid_spec=pltpu.PrefetchScalarGridSpec(
            num_scalar_prefetch=1,
            grid=(1,),
            in_specs=[whole, whole, pl.BlockSpec((codes, 2, LANES), lambda i, place: (0, 0, place[0]))],
            out_specs=pl.BlockSpec((3, 27, FREQ, LANES), lambda i, place: (0, 0, 0, 0)),
            scratch_shapes=[
                pltpu.VMEM((2, (codes // 8 + 2) * 8, LANES), jnp.float32),
                pltpu.VMEM((2, TAP_ROWS, LANES), jnp.float32),
            ],
        ),
        out_shape=jax.ShapeDtypeStruct((3, 27, FREQ, LANES), jnp.float32),
        compiler_params=pltpu.CompilerParams(vmem_limit_bytes=32 * MIB),
        cost_estimate=pl.CostEstimate(flops=1_000_000_000, bytes_accessed=MIB, transcendentals=0),
        name="table",
    )((first // LANES).reshape(1), jnp.asarray(table_matrix()), jnp.asarray(far_codes())[:, None], trans)


def upsample_kernel(places, first, own, halo, interp, cosine, sine, out, weights, held):
    tiles = out.shape[0]
    slots = own.shape[0] // LANES
    lanes = 2 * LANES

    @pl.when(pl.program_id(0) == 0)
    def _():
        weights[...] = jnp.zeros_like(weights)
        for j in range(tiles):
            for b in range(interp.shape[1]):
                start = pl.multiple_of(places[j, b] * LANES, LANES)
                weights[pl.ds(start, LANES), j * LANES : (j + 1) * LANES] = interp[first[0] + j, b]

    group = 4
    rows = group * LANES
    for i in range(slots // group):
        at = slice(i * rows, (i + 1) * rows)
        value = jnp.concatenate([own[at, :], halo[at, :]], axis=1)
        for n in range(tiles // 2):
            columns = slice(n * lanes, (n + 1) * lanes)
            u = jnp.dot(value, weights[:, columns], preferred_element_type=jnp.float32)
            u = u.reshape(group, 8, 2, 8, lanes)
            real = imag = None
            for h in range(8):
                c = cosine[h : h + 1, columns][None]
                s = sine[h : h + 1, columns][None]
                x = c * u[:, h, 0] - s * u[:, h, 1]
                y = s * u[:, h, 0] + c * u[:, h, 1]
                real, imag = (x, y) if h == 0 else (real + x, imag + y)
            kept = slice(i * group * 8, (i + 1) * group * 8)
            for t, part in enumerate((real, imag)):
                part = part.reshape(group * 8, lanes)
                held[2 * n, t, kept, :] = part[:, :LANES]
                held[2 * n + 1, t, kept, :] = part[:, LANES:]
    for tile in range(tiles):
        for t in range(2):
            for r in range(8):
                out[tile, t, r] = held[tile, t, pl.ds(r, slots, stride=8), :].astype(jnp.bfloat16)


def upsample(own, halo, interp, places, first, cosine, sine, begin, cost):
    rows = halo.shape[0]
    slots = rows // LANES
    block = min(16, slots)
    steps = slots // block
    tiles = places.shape[0]
    depth = block * LANES
    width = own.shape[1] + halo.shape[1]
    whole = pl.BlockSpec(memory_space=pltpu.VMEM)
    smem = pl.BlockSpec(memory_space=pltpu.SMEM)
    return pl.pallas_call(
        upsample_kernel,
        grid=(steps,),
        in_specs=[
            smem,
            smem,
            pl.BlockSpec((depth, own.shape[1]), lambda i: (begin // block + i, 0)),
            pl.BlockSpec((depth, halo.shape[1]), lambda i: (i, 0)),
            whole,
            whole,
            whole,
        ],
        out_specs=pl.BlockSpec((tiles, 2, 8, block, LANES), lambda i: (0, 0, 0, i, 0)),
        out_shape=pltpu.HBM((tiles, 2, 8, slots, LANES), jnp.bfloat16),
        scratch_shapes=[
            pltpu.VMEM((width, tiles * LANES), jnp.bfloat16),
            pltpu.VMEM((tiles, 2, block * 8, LANES), jnp.float32),
        ],
        compiler_params=pltpu.CompilerParams(vmem_limit_bytes=48 * MIB),
        cost_estimate=pl.CostEstimate(flops=cost, bytes_accessed=rows, transcendentals=0),
        name="upsample",
    )(places, first, own, halo, interp, cosine, sine)


def far_kernel(into, back, forward, inverse, table, *rest, count):
    ins = rest[:count]
    outs = rest[count:-4]
    moved, hat, prod, near = rest[-4:]
    grand = HALF**3
    boxes = ins[0].shape[0]
    slots = outs[0].shape[3]

    for t in range(2):
        columns = [
            jnp.concatenate([ref[box, t, r] for box in range(boxes) for ref in ins], axis=0) for r in range(2)
        ]
        rows = jnp.concatenate(columns, axis=1)
        moved[t] = jnp.dot(into[...], rows, preferred_element_type=jnp.float32).astype(jnp.bfloat16)

    for octant in range(8):
        at = slice(octant * grand, (octant + 1) * grand)
        both = jnp.concatenate([moved[0, at], moved[1, at]], axis=0)
        both = jnp.concatenate([both, both], axis=0)
        hat[octant] = jnp.dot(forward[...], both, preferred_element_type=jnp.float32)

    def products(i, carry):
        at = pl.multiple_of(i * 8, 8)
        real_at, imag_at = pl.ds(at, 8), pl.ds(FREQ + at, 8)
        for r in range(2):
            lanes = slice(r * LANES, (r + 1) * LANES)
            real = [hat[s, real_at, lanes] for s in range(8)]
            imag = [hat[s, imag_at, lanes] for s in range(8)]
            total = [a + b for a, b in zip(real, imag)]
            for t in range(8):
                sums = [None] * 3
                for s in range(8):
                    delta = 0
                    for shift in (2, 1, 0):
                        delta = delta * 3 + (s >> shift & 1) - (t >> shift & 1) + 1
                    terms = (
                        table[0, delta, real_at] * total[s],
                        table[1, delta, real_at] * real[s],
                        table[2, delta, real_at] * imag[s],
                    )
                    sums = [b if a is None else a + b for a, b in zip(sums, terms)]
                prod[t, real_at, lanes] = sums[0] - sums[2]
                prod[t, imag_at, lanes] = sums[0] + sums[1]
        return carry

    lax.fori_loop(0, FREQ // 8, products, 0)

    for octant in range(8):
        value = prod[octant]
        high = value.astype(jnp.bfloat16)
        low = (value - high.astype(jnp.float32)).astype(jnp.bfloat16)
        stacked = jnp.concatenate([high, low, high], axis=0)
        result = jnp.dot(inverse[...], stacked, preferred_element_type=jnp.float32)
        at = slice(octant * grand, (octant + 1) * grand)
        near[0, at] = result[:grand].astype(jnp.bfloat16)
        near[1, at] = result[grand:].astype(jnp.bfloat16)

    for t in range(2):
        result = jnp.dot(back[...], near[t], preferred_element_type=jnp.float32).astype(jnp.bfloat16)
        for box in range(boxes):
            ref, index = (outs[box], 0) if len(outs) > 1 else (outs[0], box)
            for r in range(2):
                ref[index, t, r] = result[box * slots : (box + 1) * slots, r * LANES : (r + 1) * LANES]


def far_field(parts, into, back, table, apart):
    boxes, _, columns, _, _ = parts[0].shape
    slots = sum(part.shape[3] for part in parts)
    parents = into.shape[0]
    whole = pl.BlockSpec(memory_space=pltpu.VMEM)

    def columnwise(boxes, rows):
        return pl.BlockSpec((boxes, 2, 2, rows, LANES), lambda i: (0, 0, i, 0, 0))

    results, each = (boxes, 1) if apart else (1, boxes)
    return pl.pallas_call(
        functools.partial(far_kernel, count=len(parts)),
        grid=(columns // 2,),
        in_specs=[whole] * 5 + [columnwise(boxes, part.shape[3]) for part in parts],
        out_specs=[columnwise(each, slots)] * results,
        out_shape=[pltpu.HBM((each, 2, columns, slots, LANES), jnp.bfloat16)] * results,
        scratch_shapes=[
            pltpu.VMEM((2, parents, 2 * LANES), jnp.bfloat16),
            pltpu.VMEM((8, 2 * FREQ, 2 * LANES), jnp.float32),
            pltpu.VMEM((8, 2 * FREQ, 2 * LANES), jnp.float32),
            pltpu.VMEM((2, parents, 2 * LANES), jnp.bfloat16),
        ],
        compiler_params=pltpu.CompilerParams(vmem_limit_bytes=48 * MIB),
        cost_estimate=pl.CostEstimate(flops=20_000_000_000, bytes_accessed=12 * MIB, transcendentals=0),
        name="far_field",
    )(into, back, jnp.asarray(forward_matrix()), jnp.asarray(inverse_matrix()), table, *parts)


def finish_kernel(side, me, *rest, tiles):
    ins = rest[:tiles]
    out, held = rest[-2:]
    slots = ins[0].shape[3]
    for s in range(tiles):
        tile = lax.rem(me[0] + tiles - s, tiles)
        for t in range(2):
            for r in range(8):
                held[tile, pl.ds(t * 8 + r, slots, stride=16), :] = ins[s][0, t, r].astype(jnp.float32)
    for tile in range(tiles):
        out[:, tile * LANES : (tile + 1) * LANES] = held[tile]


def finish(results, whole, side, me, width):
    tiles = len(results)
    _, _, _, slots, _ = results[0].shape
    block = min(16, slots)
    kept = [] if whole is None else [whole]
    return pl.pallas_call(
        functools.partial(finish_kernel, tiles=tiles),
        grid_spec=pltpu.PrefetchScalarGridSpec(
            num_scalar_prefetch=2,
            grid=(slots // block,),
            in_specs=[pl.BlockSpec((1, 2, 8, block, LANES), lambda i, *_: (0, 0, 0, i, 0))] * tiles
            + [pl.BlockSpec(memory_space=pl.ANY)] * len(kept),
            out_specs=pl.BlockSpec((block * 16, tiles * LANES), lambda i, side, me: (i, side[0])),
            scratch_shapes=[pltpu.VMEM((tiles, block * 16, LANES), jnp.float32)],
        ),
        out_shape=jax.ShapeDtypeStruct((slots * 16, width), jnp.float32),
        input_output_aliases={2 + tiles: 0} if kept else {},
        compiler_params=pltpu.CompilerParams(vmem_limit_bytes=48 * MIB),
        name="finish",
    )(side, me, *results, *kept)


def exchange(value):
    return lax.all_to_all(value, "box", 0, 0, tiled=True)


def send_apart(pieces):
    devices = len(pieces)
    moved = list(pieces)
    for s in sorted(range(1, devices), key=lambda s: abs(s - devices // 2)):
        moved[s] = lax.ppermute(pieces[s], "box", [(i, (i + s) % devices) for i in range(devices)])
    return moved


def after(value, *others):
    return lax.optimization_barrier((value, *others))[0]


def shards(child_pat, interp, interp_blocks, shift_angle, slot_parent, far_list, trans):
    boxes = lax.axis_size("box")
    box = lax.axis_index("box").astype(jnp.int32)
    directions = lax.axis_size("dir")
    here = lax.axis_index("dir").astype(jnp.int32)
    children, _, columns, width_in = child_pat.shape
    local_in = width_in // LANES
    per_center = interp.shape[0] // local_in
    total_in = local_in * directions
    slots = children // 8
    rows = children * 2 * columns
    own = child_pat.reshape(rows, width_in)
    edge = 2 * LANES

    tiles = interp.shape[0] // 2
    width = tiles * LANES
    share = width // boxes
    repeat = max(1, LANES // share)
    apart = repeat == 1
    assert local_in == 4 and directions % 2 == 0
    assert share * repeat == LANES and columns % (2 * repeat) == 0

    odd = here % 2
    inner = [(i, i + 1 - 2 * (i % 2)) for i in range(directions)]
    outer = [(i, (i + 2 * (i % 2) - 1) % directions) for i in range(directions)]
    sides = [1 - odd, odd]
    def send_edge(source, step, begin, size):
        start = (begin * LANES, sides[step] * (width_in - edge))
        send = lax.dynamic_slice(source, start, (size * LANES, edge))
        return send, lax.ppermute(send, "dir", (inner, outer)[step])

    half = slots // 2
    quarter = half // 2
    send, inner_halo = send_edge(own, 0, 0, slots)
    _, outer_first = send_edge(after(own, send), 1, 0, quarter)

    centers = jnp.arange(interp.shape[0], dtype=jnp.int32) // per_center
    window = (interp_blocks - (centers + here * local_in)[:, None] + 2) % total_in + centers[:, None] - 2

    def places_for(side):
        block = lax.dynamic_slice_in_dim(window, side * tiles, tiles, 0)
        return jnp.where(block < 0, block + local_in + 2, block)

    def pieces_of(value):
        if apart:
            return value
        slots = value.shape[3]
        value = value.reshape(tiles, 2, columns // repeat, repeat, slots, repeat, share)
        return value.transpose(0, 5, 1, 2, 4, 3, 6).reshape(boxes, 2, columns // repeat, slots, LANES)

    def tiles_of(value):
        value = value.reshape(tiles, repeat, 2, columns // repeat, slots, repeat, share)
        return value.transpose(4, 2, 3, 5, 0, 1, 6).reshape(slots, 2, columns, width).astype(jnp.float32)

    def patterns(step, halo, begin, cost):
        angle = lax.dynamic_slice_in_dim(shift_angle, sides[step] * width, width, 1)
        first = (sides[step] * tiles).reshape(1)
        cosine, sine = jnp.cos(angle), jnp.sin(angle)
        return upsample(own, halo, interp, places_for(sides[step]), first, cosine, sine, begin, cost)

    def give_back(pieces):
        return send_apart(pieces) if apart else [exchange(pieces[0])]

    value = patterns(0, inner_halo, 0, 1)
    value, outer_first = lax.optimization_barrier((value, outer_first))
    first = exchange(pieces_of(value))
    send, outer_second = send_edge(after(own, value), 1, quarter, half - quarter)

    operator, slot_parent, far_list, _ = lax.optimization_barrier((trans, slot_parent, far_list, send))
    tables = [table_of(operator, side * width + box * share, share, repeat) for side in sides]
    order = parent_order()
    listed = jnp.concatenate([far_list[row] for row in cover_rows()])
    occupied = jnp.any(listed[:, None] == order[None, :], axis=0)
    into = ((slot_parent[None, :] == order[:, None]) & occupied[:, None]).astype(jnp.bfloat16)
    leaving = slot_parent.reshape(boxes, slots)
    if apart:
        leaving = leaving[(box + jnp.arange(boxes, dtype=jnp.int32)) % boxes]
    back = (leaving.reshape(-1)[:, None] == order[None, :]).astype(jnp.bfloat16)

    _, outer_last = send_edge(after(own, *tables), 1, half, slots - half)
    halo = jnp.concatenate([outer_first, outer_second], axis=0)
    value = patterns(1, after(halo, into, back, *tables), 0, 12_000_000_000)
    second = exchange(pieces_of(value))
    pieces = far_field([after(first, value)], into, back, tables[0], apart)
    value = patterns(1, after(outer_last, pieces[0], second), half, 12_000_000_000)
    third = exchange(pieces_of(value))
    pieces = [after(piece, third) for piece in pieces]
    results = [give_back(pieces)]
    pieces = far_field([second, third], into, back, tables[1], apart)
    results.append(give_back(pieces))

    out = None
    if apart:
        for result, side in zip(results, sides):
            out = finish(result, out, side.reshape(1), box.reshape(1), 2 * width)
        return out.reshape(slots, 2, columns, 2 * width)
    first, second = (tiles_of(result[0]) for result in results)
    ordered = [jnp.where(odd == 1, first, second), jnp.where(odd == 1, second, first)]
    return jnp.concatenate(ordered, axis=-1)


def solution(mesh):
    in_specs = (
        P("box", None, None, "dir"),
        P("dir", None, None, None),
        P("dir", None),
        P(None, "dir"),
        P(),
        P(),
        P(None, None, "dir"),
    )
    out_specs = P("box", None, None, "dir")
    return jax.shard_map(shards, mesh=mesh, in_specs=in_specs, out_specs=out_specs, check_vma=False)
```
